256 devices in a mesh: row: 16 (over y, x), col: 16 (over z, core).
Axes of the slice: x: 4, y: 4, z: 8, core: 2. Of those that a mesh axis runs over, the one named last changes fastest.
Arguments:
- tokens: bfloat16 [512, 8192], P('col', 'row'), may hold values from -6 to 6
- gate_quant: bfloat16 [8192, 26624], P('row', 'col'), may hold values from -120 to 120, as said below
- gate_scale: float32 [64, 208], P('row', 'col'), as said below
- up_quant: bfloat16 [8192, 26624], P('row', 'col'), may hold values from -120 to 120, as said below
- up_scale: float32 [64, 208], P('row', 'col'), as said below
- down_quant: bfloat16 [26624, 8192], P('col', 'row'), may hold values from -120 to 120, as said below
- down_scale: float32 [208, 64], P('col', 'row'), as said below
- out_grad: bfloat16 [512, 8192], P('col', 'row'), may hold values from -6 to 6
Outputs:
- output: bfloat16 [512, 8192], P('col', 'row')
- input_grad: bfloat16 [512, 8192], P('col', 'row')
- gate_grad: bfloat16 [8192, 26624], P('row', 'col')
- up_grad: bfloat16 [8192, 26624], P('row', 'col')
- down_grad: bfloat16 [26624, 8192], P('col', 'row')
The draws below stay inside these ranges and needn't reach their ends.
Inputs may be any that keep to these rules, and one draw needn't show every extreme that they name: `gate_quant`: every entry is a sign times a mantissa of 8 to 15 eighths times a power of two from 4 to 64. `up_quant`: every entry is a sign times a mantissa of 8 to 15 eighths times a power of two from 4 to 64. `down_quant`: every entry is a sign times a mantissa of 8 to 15 eighths times a power of two from 4 to 64. `gate_scale`: every entry is a positive power of two. `up_scale`: every entry is a positive power of two. `down_scale`: every entry is a positive power of two.
All inputs are finite; a program needn't handle non-finite values.
Results may differ from the reference program's by a relative error of at most 0.005.
Values may be sent and summed in bfloat16 or wider, within the bound.
No kernel may reach another device: no remote copies, remote signals or barrier semaphores. Data moves between devices by JAX's collectives and lax.ppermute only.
A program may use at most 128 MiB of HBM per device.

```python
import math
import jax
import jax.numpy as jnp

D = 8192
FF = 26624
BLK = 128
TOKENS = 512


def grid_codes(key, shape):
    sign_key, mantissa_key, power_key = jax.random.split(key, 3)
    signs = jax.random.randint(sign_key, shape, 0, 2) * 2 - 1
    mantissa = jax.random.randint(mantissa_key, shape, 8, 16)
    powers = jax.random.randint(power_key, shape, 0, 5)
    table = jnp.array([4.0, 8.0, 16.0, 32.0, 64.0], jnp.float32)
    values = signs.astype(jnp.float32) * mantissa.astype(jnp.float32) * 0.125 * table[powers]
    return values.astype(jnp.bfloat16)


def power_scales(key, shape, fan_in):
    center = -(int(math.log2(fan_in)) // 2) - 6
    offsets = jax.random.randint(key, shape, -2, 3)
    exponents = (offsets + center).astype(jnp.float32)
    return jnp.exp2(exponents).astype(jnp.float32)


def draw_gate_quant(key, part):
    key = jax.random.fold_in(key, 11)
    return grid_codes(key, (D, FF))


def draw_up_quant(key, part):
    key = jax.random.fold_in(key, 23)
    return grid_codes(key, (D, FF))


def draw_down_quant(key, part):
    key = jax.random.fold_in(key, 37)
    return grid_codes(key, (FF, D))


def draw_gate_scale(key, part):
    key = jax.random.fold_in(key, 41)
    return power_scales(key, (D // BLK, FF // BLK), D)


def draw_up_scale(key, part):
    key = jax.random.fold_in(key, 53)
    return power_scales(key, (D // BLK, FF // BLK), D)


def draw_down_scale(key, part):
    key = jax.random.fold_in(key, 67)
    return power_scales(key, (FF // BLK, D // BLK), FF)


def steps_of(rng, extent, cuts, least, high):
    gain = 1.0
    for axis_at, blocks in cuts:
        draws = jax.random.uniform(jax.random.fold_in(jax.random.fold_in(rng, 6), axis_at), (blocks,), jnp.float32, least / len(cuts), high / len(cuts))
        gain = gain * jnp.repeat(jnp.exp(draws), extent[axis_at] // blocks).reshape((-1,) + (1,) * (len(extent) - 1 - axis_at))
    return gain


def centred(own_key, dims, deviation, bound, cuts=(), kind=jnp.bfloat16):
    values = jax.random.normal(own_key, dims, jnp.float32) * deviation
    if len(cuts) > 0:
        values = steps_of(own_key, dims, cuts, -0.22, 0.18) * values
    return jnp.clip(values, min=-bound, max=bound).astype(kind)


def setup_inputs(seed: int = 0) -> dict:
    streams_of = jax.random.split(jax.random.key(seed), 9)
    tokens = centred(streams_of[0], (TOKENS, D), 1.0, 6.0, ((0, 16), (1, 16)))
    gate_quant = draw_gate_quant(jax.random.fold_in(streams_of[8], 71), 0)
    gate_scale = draw_gate_scale(jax.random.fold_in(streams_of[8], 71), 0)
    up_quant = draw_up_quant(jax.random.fold_in(streams_of[8], 71), 0)
    up_scale = draw_up_scale(jax.random.fold_in(streams_of[8], 71), 0)
    down_quant = draw_down_quant(jax.random.fold_in(streams_of[8], 71), 0)
    down_scale = draw_down_scale(jax.random.fold_in(streams_of[8], 71), 0)
    out_grad = centred(streams_of[7], (TOKENS, D), 1.0, 6.0, ((0, 16), (1, 16)))
    return {"tokens": tokens, "gate_quant": gate_quant, "gate_scale": gate_scale, "up_quant": up_quant, "up_scale": up_scale, "down_quant": down_quant, "down_scale": down_scale, "out_grad": out_grad}


def dequantize(quantized, scales):
    block_rows, block_columns = scales.shape
    height, width = quantized.shape
    blocks = quantized.astype(jnp.float32).reshape(block_rows, height // block_rows, block_columns, width // block_columns)
    return (blocks * scales[:, None, :, None]).reshape(height, width).astype(jnp.bfloat16)


def reference(tokens, gate_quant, gate_scale, up_quant, up_scale, down_quant, down_scale, out_grad):
    w_gate = dequantize(gate_quant, gate_scale)
    w_up = dequantize(up_quant, up_scale)
    w_down = dequantize(down_quant, down_scale)
    gate = jnp.dot(tokens, w_gate, preferred_element_type=jnp.float32)
    up = jnp.dot(tokens, w_up, preferred_element_type=jnp.float32)
    sigmoid_gate = jax.nn.sigmoid(gate)
    activated = gate * sigmoid_gate
    hidden = (activated * up).astype(jnp.bfloat16)
    output = jnp.dot(hidden, w_down, preferred_element_type=jnp.float32).astype(jnp.bfloat16)
    down_grad = jnp.dot(hidden.T, out_grad, preferred_element_type=jnp.float32).astype(jnp.bfloat16)
    hidden_grad = jnp.dot(out_grad, w_down.T, preferred_element_type=jnp.float32)
    pre_gate = (hidden_grad * up * sigmoid_gate * (1.0 + gate * (1.0 - sigmoid_gate))).astype(jnp.bfloat16)
    pre_up = (hidden_grad * activated).astype(jnp.bfloat16)
    gate_grad = jnp.dot(tokens.T, pre_gate, preferred_element_type=jnp.float32).astype(jnp.bfloat16)
    up_grad = jnp.dot(tokens.T, pre_up, preferred_element_type=jnp.float32).astype(jnp.bfloat16)
    input_grad = jnp.dot(pre_gate, w_gate.T, preferred_element_type=jnp.float32) + jnp.dot(pre_up, w_up.T, preferred_element_type=jnp.float32)
    return output, input_grad.astype(jnp.bfloat16), gate_grad, up_grad, down_grad
```

```python
import jax
import jax.numpy as jnp
from jax import lax
from jax.experimental import pallas as pl
from jax.experimental.pallas import tpu as pltpu
from jax.sharding import PartitionSpec as P

F32 = jnp.float32
BF16 = jnp.bfloat16
F16 = jnp.float16
BOTH = ("row", "col")

GRAY_A = (0, 1, 1, 0)
GRAY_B = (0, 0, 1, 1)
SPLIT = 896
TAIL = 16
FIRST = (3, 2, 1, 0)
SECOND = (2, 3, 0, 1)


def code_of(y, x, core):
    along_x = 2 * GRAY_A[x] + GRAY_B[x]
    along_y = 2 * GRAY_A[y] + GRAY_B[y]
    return 4 * along_x + along_y if core == 0 else 4 * along_y + along_x


PLACE = {
    (code_of(y, x, core), core): y * 4 + x
    for y in range(4)
    for x in range(4)
    for core in range(2)
}


def flips(bit):
    pairs = []
    for row in range(16):
        for col in range(16):
            code = code_of(row // 4, row % 4, col % 2)
            pairs.append((row * 16 + col, PLACE[(code ^ (1 << bit), col % 2)] * 16 + col))
    return pairs


FLIPS = tuple(flips(bit) for bit in range(4))
CORES = [(i, i ^ 1) for i in range(16)]


def swap_bits(j):
    return ((j >> 2) & 1) << 3 | ((j >> 3) & 1) << 2 | (j & 1) << 1 | ((j >> 1) & 1)


def dequantize(quantized, scales):
    block_rows, block_columns = scales.shape
    height, width = quantized.shape
    blocks = quantized.astype(F32).reshape(
        block_rows, height // block_rows, block_columns, width // block_columns
    )
    return (blocks * scales[:, None, :, None]).reshape(height, width).astype(BF16)


def mm(left, right):
    return lax.dot_general(left, right, (((1,), (0,)), ((), ())), preferred_element_type=F32)


def mm_nt(left, right):
    return lax.dot_general(left, right, (((1,), (1,)), ((), ())), preferred_element_type=F32)


def mm_tn(left, right):
    return lax.dot_general(left, right, (((0,), (0,)), ((), ())), preferred_element_type=F32)


def reorder_kernel(count, index_ref, x_ref, o_ref):
    height = o_ref.shape[0] // count
    for j in range(count):
        start = pl.multiple_of(index_ref[j] * height, height)
        o_ref[pl.ds(j * height, height), :] = x_ref[pl.ds(start, height), :]


def reorder(x, index):
    count = index.shape[0]
    height = x.shape[0] // 16
    return pl.pallas_call(
        lambda *refs: reorder_kernel(count, *refs),
        out_shape=jax.ShapeDtypeStruct((count * height, x.shape[1]), x.dtype),
        in_specs=[
            pl.BlockSpec(memory_space=pltpu.SMEM),
            pl.BlockSpec(memory_space=pltpu.VMEM),
        ],
        out_specs=pl.BlockSpec(memory_space=pltpu.VMEM),
    )(index, x)


def swap_rows(x):
    width = x.shape[1]
    height = x.shape[0] // 16
    return (
        x.reshape(2, 2, 2, 2, height, width).transpose(1, 0, 3, 2, 4, 5).reshape(16 * height, width)
    )


def start_sum(total):
    peak = jnp.max(jnp.abs(total), axis=0, keepdims=True)
    power = jnp.ceil(jnp.log2(jnp.maximum(peak, 1e-36))) - 10.0
    return total, jnp.clip(power, -100.0, 118.0)


def halve(total, power, bit):
    half = total.shape[0] // 2
    scaled = (total[half:] * jnp.exp2(-power)).astype(F16)
    tail = jnp.broadcast_to(power.astype(F16), (TAIL, power.shape[1]))
    came = lax.ppermute(jnp.concatenate([scaled, tail], axis=0), BOTH, FLIPS[bit])
    other = came[half : half + 1].astype(F32)
    return total[:half] + came[:half].astype(F32) * jnp.exp2(other), jnp.maximum(power, other)


def double(parts, bits):
    for bit in bits[::-1]:
        parts = jnp.concatenate([parts, lax.ppermute(parts, BOTH, FLIPS[bit])], axis=0)
    return parts


def local(tokens, gate_quant, gate_scale, up_quant, up_scale, down_quant, down_scale, out_grad):
    row = lax.axis_index("row")
    col = lax.axis_index("col")
    core = lax.rem(col, 2)
    depth = lax.div(col, 2)
    table = jnp.array(
        [[code_of(r // 4, r % 4, c) for c in range(2)] for r in range(16)], jnp.int32
    )
    code = table[row, core]
    blocks = jnp.arange(16, dtype=jnp.int32)
    index_a = jnp.bitwise_xor(blocks, code)
    index_b = jnp.bitwise_xor(jnp.array([swap_bits(j) for j in range(16)], jnp.int32), code)
    turn = lax.rem(depth + jnp.arange(8, dtype=jnp.int32), 8) * 2
    index_keep = jnp.bitwise_xor(turn + core, code)
    index_give = jnp.bitwise_xor(turn + (1 - core), code)

    w_gate = dequantize(gate_quant, gate_scale)
    w_up = dequantize(up_quant, up_scale)
    w_down = dequantize(down_quant, down_scale)

    panel = lax.all_gather(tokens, "col", axis=0, tiled=True)
    tokens_a = reorder(panel, index_a)
    tokens_b = reorder(panel, index_b)
    gate, gate_power = start_sum(mm(tokens_a, w_gate))
    up, up_power = start_sum(mm(tokens_b, w_up))
    gate, gate_power = halve(gate, gate_power, FIRST[0])
    up, up_power = halve(up, up_power, SECOND[0])

    grad_panel = lax.all_gather(out_grad, "col", axis=0, tiled=True)
    grads_a = reorder(grad_panel, index_a)
    grads_b = reorder(grad_panel, index_b)
    back_a, back_a_power = start_sum(mm_nt(grads_a, w_down[:SPLIT]))
    back_b, back_b_power = start_sum(mm_nt(grads_b, w_down[SPLIT:]))
    for step in range(1, 4):
        gate, gate_power = halve(gate, gate_power, FIRST[step])
        up, up_power = halve(up, up_power, SECOND[step])
    for step in range(4):
        back_a, back_a_power = halve(back_a, back_a_power, FIRST[step])
        back_b, back_b_power = halve(back_b, back_b_power, SECOND[step])
    hidden_grad = jnp.concatenate([back_a, back_b], axis=1)

    sigmoid_gate = jax.nn.sigmoid(gate)
    activated = gate * sigmoid_gate
    hidden = (activated * up).astype(BF16)
    hidden_a = double(hidden[:, :SPLIT], FIRST)
    hidden_b = double(hidden[:, SPLIT:], SECOND)
    output = mm(hidden_a, w_down[:SPLIT]) + swap_rows(mm(hidden_b, w_down[SPLIT:]))
    down_grad = jnp.concatenate(
        [mm_tn(hidden_a, grads_a).astype(BF16), mm_tn(hidden_b, grads_b).astype(BF16)], axis=0
    )

    pre_gate = (hidden_grad * up * sigmoid_gate * (1.0 + gate * (1.0 - sigmoid_gate))).astype(BF16)
    pre_up = (hidden_grad * activated).astype(BF16)
    pre_gate = double(pre_gate, FIRST)
    pre_up = double(pre_up, SECOND)
    gate_grad = mm_tn(tokens_a, pre_gate).astype(BF16)
    up_grad = mm_tn(tokens_b, pre_up).astype(BF16)
    input_grad = mm_nt(pre_gate, w_gate) + swap_rows(mm_nt(pre_up, w_up))

    def finish(total):
        keep = reorder(total, index_keep)
        came = lax.ppermute(reorder(total, index_give), "col", CORES)
        pair = keep + came
        sent = pair.astype(BF16)
        result = pair[:32]
        for shift in range(1, 8):
            moved = lax.ppermute(
                sent[32 * shift : 32 * shift + 32],
                "col",
                [(i, (i + 2 * shift) % 16) for i in range(16)],
            )
            result = result + moved.astype(F32)
        return result.astype(BF16)

    return (finish(output), finish(input_grad), gate_grad, up_grad, down_grad)


def solution(mesh):
    placed = (
        P("col", "row"),
        P("row", "col"),
        P("row", "col"),
        P("row", "col"),
        P("row", "col"),
        P("col", "row"),
        P("col", "row"),
        P("col", "row"),
    )
    return jax.shard_map(
        local,
        mesh=mesh,
        in_specs=placed,
        out_specs=(
            P("col", "row"),
            P("col", "row"),
            P("row", "col"),
            P("row", "col"),
            P("col", "row"),
        ),
        check_vma=False,
    )
```

```python
import jax
import jax.numpy as jnp
from jax import lax
from jax.experimental import pallas as pl
from jax.experimental.pallas import tpu as pltpu
from jax.sharding import PartitionSpec as P

F32 = jnp.float32
BF16 = jnp.bfloat16
BOTH = ("row", "col")


GRAY_A = (0, 1, 1, 0)
GRAY_B = (0, 0, 1, 1)
WIDE = 1664
SPLIT = 896
PART_A = WIDE + SPLIT
PART_B = WIDE + WIDE - SPLIT
LIMIT = 40 * 1024 * 1024


def code_of(y, x, core):
    along_x = 2 * GRAY_A[x] + GRAY_B[x]
    along_y = 2 * GRAY_A[y] + GRAY_B[y]
    return 4 * along_x + along_y if core == 0 else 4 * along_y + along_x


PLACE = {
    (code_of(y, x, core), core): y * 4 + x
    for y in range(4)
    for x in range(4)
    for core in range(2)
}


def flips(mask):
    pairs = []
    for row in range(16):
        for col in range(16):
            code = code_of(row // 4, row % 4, col % 2)
            pairs.append((row * 16 + col, PLACE[(code ^ mask, col % 2)] * 16 + col))
    return pairs


FLIPS = {mask: flips(mask) for mask in (1, 2, 3, 4, 8)}
CORES = [(i, i ^ 1) for i in range(16)]


def turn_by(shift):
    return [(i, (i + 2 * shift) % 16) for i in range(16)]


def swap_bits(j):
    return (j & 3) | ((j >> 2) & 1) << 3 | ((j >> 3) & 1) << 2


def send(x, mask):
    return lax.ppermute(x, BOTH, FLIPS[mask])


def tiles(start, stop):
    return [(at, min(at + 256, stop)) for at in range(start, stop, 256)]


def nn(left, right):
    return lax.dot_general(left, right, (((1,), (0,)), ((), ())), preferred_element_type=F32)


def nt(left, right):
    return lax.dot_general(left, right, (((1,), (1,)), ((), ())), preferred_element_type=F32)


def tn(left, right):
    return lax.dot_general(left, right, (((0,), (0,)), ((), ())), preferred_element_type=F32)


def run(kernel, outs, arrays, smem=0, scratch=(), flops=0):
    moved = sum(a.size * a.dtype.itemsize for a in arrays)
    shapes = [jax.ShapeDtypeStruct(shape, kind) for shape, kind in outs]
    moved += sum(s.size * s.dtype.itemsize for s in shapes)
    specs = [pl.BlockSpec(memory_space=pltpu.SMEM)] * smem
    specs += [pl.BlockSpec(memory_space=pltpu.VMEM)] * (len(arrays) - smem)
    return pl.pallas_call(
        kernel,
        out_shape=shapes,
        in_specs=specs,
        out_specs=[pl.BlockSpec(memory_space=pltpu.VMEM)] * len(shapes),
        scratch_shapes=list(scratch),
        compiler_params=pltpu.CompilerParams(vmem_limit_bytes=LIMIT),
        cost_estimate=pl.CostEstimate(flops=flops, bytes_accessed=moved, transcendentals=0),
    )(*arrays)


def arrange(index, panel, out):
    for part in range(2):
        for j in range(16):
            start = pl.multiple_of(index[j] * 32 + part * 16, 16)
            out[pl.ds(part * 256 + j * 16, 16), :] = panel[pl.ds(start, 16), :]


def scale_blocks(quant, scale, weight):
    block_rows, block_columns = scale.shape
    for r in range(block_rows):
        for c in range(block_columns):
            rows, columns = pl.ds(r * 128, 128), pl.ds(c * 128, 128)
            weight[rows, columns] = (quant[rows, columns].astype(F32) * scale[r, c]).astype(BF16)


def deal(product, at, stop, keep0, give0, keep1, give1):
    keep0[:, at:stop] = product[:128]
    give0[:, at:stop] = product[128:256].astype(BF16)
    keep1[:, at:stop] = product[256:384]
    give1[:, at:stop] = product[384:].astype(BF16)


def forward_kernel(index, scale, panel, quant, arranged, weight, *parts):
    arrange(index, panel, arranged)
    scale_blocks(quant, scale, weight)
    for at, stop in tiles(0, WIDE):
        deal(nn(arranged[...], weight[:, at:stop]), at, stop, *parts)


def parts_of(width):
    return [((128, width), F32), ((128, width), BF16)] * 2


def forward(index, scale, panel, quant):
    outs = [((512, 512), BF16), ((512, WIDE), BF16)] + parts_of(WIDE)
    return run(
        forward_kernel, outs, [index, scale, panel, quant], smem=2, flops=2 * 512 * 512 * WIDE
    )


def backward_kernel(index_a, index_b, scale, panel, quant, arranged_a, arranged_b, weight, *parts):
    arrange(index_a, panel, arranged_a)
    arrange(index_b, panel, arranged_b)
    scale_blocks(quant, scale, weight)
    for at, stop in tiles(0, SPLIT):
        deal(nt(arranged_a[...], weight[at:stop, :]), at, stop, *parts[:4])
    for at, stop in tiles(SPLIT, WIDE):
        deal(nt(arranged_b[...], weight[at:stop, :]), at - SPLIT, stop - SPLIT, *parts[4:])


def backward(index_a, index_b, scale, panel, quant):
    outs = [((512, 512), BF16)] * 2 + [((WIDE, 512), BF16)]
    outs += parts_of(SPLIT) + parts_of(WIDE - SPLIT)
    return run(
        backward_kernel,
        outs,
        [index_a, index_b, scale, panel, quant],
        smem=3,
        flops=2 * 512 * 512 * WIDE,
    )


def second_kernel(*refs):
    ins, (keep_a, give_a, keep_b, give_b) = refs[:8], refs[8:]
    for at, (held, came, keep, give) in (
        (0, (*ins[0:2], keep_a, give_a)),
        (WIDE, (*ins[2:4], keep_a, give_a)),
        (0, (*ins[4:6], keep_b, give_b)),
        (WIDE, (*ins[6:8], keep_b, give_b)),
    ):
        width = held.shape[1]
        keep[:, at : at + width] = held[:64] + came[:64].astype(F32)
        give[:, at : at + width] = held[64:] + came[64:].astype(F32)


def second(*arrays):
    outs = [((64, PART_A), F32)] * 2 + [((64, PART_B), F32)] * 2
    return run(second_kernel, outs, arrays)


def third_kernel(held_a, came_a, held_b, came_b, *outs):
    for j in range(4):
        rows = pl.ds(16 * j, 16)
        outs[j][:, :PART_A] = held_a[rows, :] + came_a[rows, :]
        outs[j][:, PART_A:] = held_b[rows, :] + came_b[rows, :]


def third(*arrays):
    return run(third_kernel, [((16, PART_A + PART_B), F32)] * 4, arrays)


def middle_kernel(held, came_1, came_2, came_3, out):
    def total(at, stop):
        return (held[:, at:stop] + came_1[:, at:stop]) + (came_2[:, at:stop] + came_3[:, at:stop])

    for at, stop in [(0, SPLIT), (SPLIT, WIDE)]:
        gate = total(at, stop)
        up = total(PART_A + at, PART_A + stop)
        offset = WIDE if at == 0 else PART_A + WIDE - SPLIT
        back = total(offset + at, offset + stop)
        sigmoid = 1.0 / (1.0 + jnp.exp(-gate))
        activated = gate * sigmoid
        out[:, offset + at : offset + stop] = (activated * up).astype(BF16)
        slope = sigmoid * (1.0 + gate * (1.0 - sigmoid))
        out[:, at:stop] = (back * up * slope).astype(BF16)
        out[:, PART_A + at : PART_A + stop] = (back * activated).astype(BF16)


def middle(*arrays):
    return run(middle_kernel, [((16, PART_A + PART_B), BF16)], arrays)[0]


def spread_kernel(*refs):
    ins, (out_a, out_b) = refs[:4], refs[4:]
    for j in range(4):
        out_a[pl.ds(16 * j, 16), :] = ins[j][:, :PART_A]
        out_b[pl.ds(16 * j, 16), :] = ins[j][:, PART_A:]


def spread(*arrays):
    return run(spread_kernel, [((64, PART_A), BF16), ((64, PART_B), BF16)], arrays)


def join_kernel(a, came_a, b, came_b, out_a, out_b):
    out_a[:64, :] = a[...]
    out_a[64:, :] = came_a[...]
    out_b[:64, :] = b[...]
    out_b[64:, :] = came_b[...]


def join(*arrays):
    return run(join_kernel, [((128, PART_A), BF16), ((128, PART_B), BF16)], arrays)


def project_kernel(index_a, index_b, a, came_a, b, came_b, gate, up, down, keep, give, sum_a, sum_b):
    for rows, left, right in ((0, a, b), (128, came_a, came_b)):
        at = pl.ds(rows, 128)
        sum_a[at, :512] = nn(left[:, WIDE:], down[:SPLIT, :])
        sum_b[at, :512] = nn(right[:, WIDE:], down[SPLIT:, :])
        sum_a[at, 512:] = nt(left[:, :WIDE], gate[...])
        sum_b[at, 512:] = nt(right[:, :WIDE], up[...])
    for k in range(16):
        out = keep if k < 8 else give
        from_a = pl.multiple_of(index_a[k] * 16, 16)
        from_b = pl.multiple_of(index_b[k] * 16, 16)
        out[pl.ds((k % 8) * 16, 16), :] = (
            sum_a[pl.ds(from_a, 16), :] + sum_b[pl.ds(from_b, 16), :]
        )


def project(*arrays):
    return run(
        project_kernel,
        [((128, 1024), F32)] * 2,
        arrays,
        smem=2,
        scratch=[pltpu.VMEM((256, 1024), F32)] * 2,
        flops=3 * 2 * 256 * 512 * WIDE,
    )


def chunk_kernel(keep_0, came_0, keep_1, came_1, own, *outs):
    for k in range(8):
        rows = pl.ds(16 * k, 16)
        out = own if k == 0 else outs[k - 1]
        out[:16, :] = (keep_0[rows, :] + came_0[rows, :]).astype(out.dtype)
        out[16:, :] = (keep_1[rows, :] + came_1[rows, :]).astype(out.dtype)


def chunk(*arrays):
    return run(chunk_kernel, [((32, 1024), F32)] + [((32, 1024), BF16)] * 7, arrays)


def finish_kernel(own, *refs):
    total = own[...]
    for came in refs[:7]:
        total = total + came[...].astype(F32)
    refs[7][...] = total[:, :512].astype(BF16)
    refs[8][...] = total[:, 512:].astype(BF16)


def finish(*arrays):
    return run(finish_kernel, [((32, 512), BF16)] * 2, arrays)


def wide_grad_kernel(panel, first, second, third, fourth, out):
    for at, stop in tiles(0, WIDE):
        pieces = [part[:, at:stop] for part in (first, second, third, fourth)]
        out[:, at:stop] = tn(panel[...], jnp.concatenate(pieces, axis=0)).astype(BF16)


def wide_grad(*arrays):
    return run(wide_grad_kernel, [((512, WIDE), BF16)], arrays, flops=2 * 512 * 512 * WIDE)[0]


def down_grad_kernel(panel_a, panel_b, *refs):
    out = refs[8]
    for panel, parts, offset, stop_at in (
        (panel_a, refs[:4], 0, SPLIT),
        (panel_b, refs[4:8], SPLIT, WIDE),
    ):
        for at, stop in tiles(offset, stop_at):
            shift = WIDE - offset
            pieces = [part[:, at + shift : stop + shift] for part in parts]
            out[at:stop, :] = tn(jnp.concatenate(pieces, axis=0), panel[...]).astype(BF16)


def down_gradient(*arrays):
    return run(down_grad_kernel, [((WIDE, 512), BF16)], arrays, flops=2 * 512 * 512 * WIDE)[0]


def local(tokens, gate_quant, gate_scale, up_quant, up_scale, down_quant, down_scale, out_grad):
    row = lax.axis_index("row")
    col = lax.axis_index("col")
    core = lax.rem(col, 2)
    depth = lax.div(col, 2)
    table = jnp.array(
        [[code_of(r // 4, r % 4, c) for c in range(2)] for r in range(16)], jnp.int32
    )
    code = table[row, core]
    blocks = jnp.arange(16, dtype=jnp.int32)

    def swapped(j):
        return (j & 3) | (((j >> 2) & 1) << 3) | (((j >> 3) & 1) << 2)

    index_a = blocks ^ code
    index_b = swapped(blocks) ^ code
    turn = lax.rem(depth + blocks % 8, 8) * 2
    home_a = (turn + jnp.where(blocks < 8, core, 1 - core)) ^ code
    home_b = swapped(home_a)

    panel = lax.all_gather(tokens, "col", axis=0, tiled=True)
    tokens_b, w_up, up_0, up_give_0, up_1, up_give_1 = forward(index_b, up_scale, panel, up_quant)
    up_came_0, up_came_1 = send(up_give_0, 4), send(up_give_1, 4)
    tokens_a, w_gate, gate_0, gate_give_0, gate_1, gate_give_1 = forward(
        index_a, gate_scale, panel, gate_quant
    )
    gate_came_0, gate_came_1 = send(gate_give_0, 8), send(gate_give_1, 8)

    grad_panel = lax.all_gather(out_grad, "col", axis=0, tiled=True)
    grads_a, grads_b, w_down, *back = backward(
        index_a, index_b, down_scale, grad_panel, down_quant
    )
    state = []
    for part, held in enumerate(
        ((gate_0, gate_came_0, up_0, up_came_0), (gate_1, gate_came_1, up_1, up_came_1))
    ):
        keep_a, give_a = back[2 * part : 2 * part + 2]
        keep_b, give_b = back[4 + 2 * part : 6 + 2 * part]
        state.append(
            (*held[:2], keep_a, send(give_a, 8), *held[2:], keep_b, send(give_b, 4))
        )
    for part in range(2):
        keep_a, give_a, keep_b, give_b = second(*state[part])
        state[part] = (keep_a, send(give_a, 4), keep_b, send(give_b, 8))
    for part in range(2):
        held, *give = third(*state[part])
        state[part] = (held, *(send(give[j - 1], j) for j in (1, 2, 3)))
    for part in range(2):
        own = middle(*state[part])
        state[part] = (own, *(send(own, j) for j in (1, 2, 3)))
    for part in range(2):
        a, b = spread(*state[part])
        state[part] = (a, send(a, 4), b, send(b, 8))
    for part in range(2):
        a, b = join(*state[part])
        state[part] = (a, send(a, 8), b, send(b, 4))
    ends = []
    for part in range(2):
        keep, give = project(home_a, home_b, *state[part], w_gate, w_up, w_down)
        ends += [keep, lax.ppermute(give, "col", CORES)]
    own, *sent = chunk(*ends)
    output, input_grad = finish(
        own, *(lax.ppermute(sent[k - 1], "col", turn_by(k)) for k in range(1, 8))
    )
    all_a = [*state[0][:2], *state[1][:2]]
    all_b = [*state[0][2:], *state[1][2:]]
    gate_grad = wide_grad(tokens_a, *all_a)
    up_grad = wide_grad(tokens_b, *all_b)
    down_grad = down_gradient(grads_a, grads_b, *all_a, *all_b)
    return (output, input_grad, gate_grad, up_grad, down_grad)


def solution(mesh):
    placed = (
        P("col", "row"),
        P("row", "col"),
        P("row", "col"),
        P("row", "col"),
        P("row", "col"),
        P("col", "row"),
        P("col", "row"),
        P("col", "row"),
    )
    return jax.shard_map(
        local,
        mesh=mesh,
        in_specs=placed,
        out_specs=(
            P("col", "row"),
            P("col", "row"),
            P("row", "col"),
            P("row", "col"),
            P("col", "row"),
        ),
        check_vma=False,
    )
```

```python
import math

import jax
import jax.numpy as jnp
from jax import lax
from jax.experimental import pallas as pl
from jax.experimental.pallas import tpu as pltpu
from jax.sharding import PartitionSpec as P

F32 = jnp.float32
BF16 = jnp.bfloat16
BOTH = ("row", "col")


GRAY_A = (0, 1, 1, 0)
GRAY_B = (0, 0, 1, 1)
WIDE = 1664
SPLIT = 896
PART_A = WIDE + SPLIT
PART_B = WIDE + WIDE - SPLIT
ROOM = 6 * 1024 * 1024


def code_of(y, x, core):
    along_x = 2 * GRAY_A[x] + GRAY_B[x]
    along_y = 2 * GRAY_A[y] + GRAY_B[y]
    return 4 * along_x + along_y if core == 0 else 4 * along_y + along_x


PLACE = {
    (code_of(y, x, core), core): y * 4 + x
    for y in range(4)
    for x in range(4)
    for core in range(2)
}


def flips(mask):
    pairs = []
    for row in range(16):
        for col in range(16):
            code = code_of(row // 4, row % 4, col % 2)
            pairs.append((row * 16 + col, PLACE[(code ^ mask, col % 2)] * 16 + col))
    return pairs


FLIPS = {mask: flips(mask) for mask in (1, 2, 3, 4, 8)}
CORES = [(i, i ^ 1) for i in range(16)]


def turn_by(shift):
    return [(i, (i + 2 * shift) % 16) for i in range(16)]


def fan_by(shift):
    return [(i, (i + (2 - 4 * (i % 2)) * shift) % 16) for i in range(16)]


def send(x, mask):
    return lax.ppermute(x, BOTH, FLIPS[mask])


def tiles(start, stop):
    return [(at, min(at + 256, stop)) for at in range(start, stop, 256)]


def nn(left, right):
    return lax.dot_general(left, right, (((1,), (0,)), ((), ())), preferred_element_type=F32)


def tn(left, right):
    return lax.dot_general(left, right, (((0,), (0,)), ((), ())), preferred_element_type=F32)


def run(kernel, outs, arrays, smem=0, far=(), scratch=(), flops=0):
    shapes = [jax.ShapeDtypeStruct(shape, kind) for shape, kind in outs]
    moved = sum(math.prod(a.shape) * a.dtype.itemsize for a in (*arrays, *shapes))
    held = moved + sum(
        math.prod(s.shape) * jnp.dtype(s.dtype).itemsize for s in scratch if len(s.shape) > 1
    )
    places = [pltpu.SMEM if k < smem else pltpu.VMEM for k in range(len(arrays) + len(outs))]
    for k in far:
        places[k] = pl.ANY
    specs = [pl.BlockSpec(memory_space=place) for place in places]
    return pl.pallas_call(
        kernel,
        out_shape=shapes,
        in_specs=specs[: len(arrays)],
        out_specs=specs[len(arrays) :],
        scratch_shapes=list(scratch),
        compiler_params=pltpu.CompilerParams(vmem_limit_bytes=held + ROOM),
        cost_estimate=pl.CostEstimate(flops=flops, bytes_accessed=moved, transcendentals=0),
    )(*arrays)


def stack_kernel(*refs):
    at = 0
    for ref in refs[:-1]:
        refs[-1][pl.ds(at, ref.shape[0]), :] = ref[...]
        at += ref.shape[0]


def stack(*arrays):
    height = sum(a.shape[0] for a in arrays)
    return run(stack_kernel, [((height, arrays[0].shape[1]), arrays[0].dtype)], arrays)[0]


def pair_kernel(both, other, out):
    for which in range(2):
        rows = pl.ds(32 * which, 32)
        out[pl.ds(64 * which, 32), :] = both[rows, :]
        out[pl.ds(64 * which + 32, 32), :] = other[rows, :]


def pair_up(*arrays):
    return run(pair_kernel, [((128, 512), BF16)], arrays)[0]


def arrange_kernel(index_a, index_b, pair, near_1, near_2, near_3, four, post, *refs):
    outs, panel = refs[:-1], refs[-1]
    for which in range(2):
        here = 64 * which
        for slot, ref in enumerate((pair, near_1, near_2, near_3)):
            panel[pl.ds(64 * slot, 64), :] = ref[pl.ds(here, 64), :]
        panel[pl.ds(256, 32), :] = four[pl.ds(32 * which, 32), :]
        panel[pl.ds(288, 32), :] = post[pl.ds(384 + 32 * which, 32), :]
        for k in (1, 2, 3):
            at, start = 64 * (8 - k), 128 * (k - 1) + here
            panel[pl.ds(at + 32, 32), :] = post[pl.ds(start, 32), :]
            panel[pl.ds(at, 32), :] = post[pl.ds(start + 32, 32), :]
        for index, out in zip((index_a, index_b), outs[2 * which : 2 * which + 2]):
            for part in range(2):
                for j in range(16):
                    start = pl.multiple_of(index[j] * 32 + part * 16, 16)
                    out[pl.ds(part * 256 + j * 16, 16), :] = panel[pl.ds(start, 16), :]


def arrange(*arrays):
    return run(
        arrange_kernel,
        [((512, 512), BF16)] * 4,
        arrays,
        smem=2,
        scratch=[pltpu.VMEM((512, 512), BF16)],
    )


def scale_kernel(scale, quant, weight, turned):
    block_rows, block_columns = scale.shape
    for r in range(block_rows):
        for c in range(block_columns):
            rows, columns = pl.ds(r * 128, 128), pl.ds(c * 128, 128)
            block = (quant[rows, columns].astype(F32) * scale[r, c]).astype(BF16)
            weight[rows, columns] = block
            turned[columns, rows] = jnp.transpose(block)


def scaled(scale, quant):
    outs = [(quant.shape, BF16), (quant.shape[::-1], BF16)]
    return run(scale_kernel, outs, [scale, quant], smem=1)


def first_kernel(tokens_a, tokens_b, grads_a, grads_b, gate, up, down, *outs):
    a, b = outs[:4], outs[4:]
    for panel, weight, first, last, shift, (keep_0, give_0, keep_1, give_1) in (
        (tokens_a, gate, 0, WIDE, 0, a),
        (tokens_b, up, 0, WIDE, 0, b),
        (grads_a, down, 0, SPLIT, WIDE, a),
        (grads_b, down, SPLIT, WIDE, WIDE - SPLIT, b),
    ):
        for at, stop in tiles(first, last):
            product = nn(panel[...], weight[:, at:stop])
            columns = pl.ds(at + shift, stop - at)
            keep_0[:, columns] = product[:128]
            give_0[:, columns] = product[128:256].astype(BF16)
            keep_1[:, columns] = product[256:384]
            give_1[:, columns] = product[384:].astype(BF16)


def first(*arrays):
    outs = []
    for width in (PART_A, PART_B):
        outs += [((128, width), F32), ((128, width), BF16)] * 2
    return run(first_kernel, outs, arrays, flops=3 * 2 * 512 * 512 * WIDE)


def second_kernel(held_a, came_a, held_b, came_b, keep_a, give_a, keep_b, give_b):
    for held, came, keep, give in (
        (held_a, came_a, keep_a, give_a),
        (held_b, came_b, keep_b, give_b),
    ):
        keep[...] = held[:64] + came[:64].astype(F32)
        give[...] = (held[64:] + came[64:].astype(F32)).astype(give.dtype)


def second(*arrays):
    outs = [((64, width), kind) for width in (PART_A, PART_B) for kind in (F32, BF16)]
    return run(second_kernel, outs, arrays)


def third_kernel(held_a, came_a, held_b, came_b, *outs):
    for j in range(4):
        rows = pl.ds(16 * j, 16)
        outs[j][:, :PART_A] = held_a[rows, :] + came_a[rows, :].astype(F32)
        outs[j][:, PART_A:] = held_b[rows, :] + came_b[rows, :].astype(F32)


def third(*arrays):
    return run(third_kernel, [((16, PART_A + PART_B), F32)] * 4, arrays)


def middle_kernel(held, came_1, came_2, came_3, out):
    def total(at, stop):
        return (held[:, at:stop] + came_1[:, at:stop]) + (came_2[:, at:stop] + came_3[:, at:stop])

    for at, stop in [(0, SPLIT), (SPLIT, WIDE)]:
        gate = total(at, stop)
        up = total(PART_A + at, PART_A + stop)
        offset = WIDE if at == 0 else PART_A + WIDE - SPLIT
        back = total(offset + at, offset + stop)
        sigmoid = 1.0 / (1.0 + jnp.exp(-gate))
        activated = gate * sigmoid
        out[:, offset + at : offset + stop] = (activated * up).astype(BF16)
        slope = sigmoid * (1.0 + gate * (1.0 - sigmoid))
        out[:, at:stop] = (back * up * slope).astype(BF16)
        out[:, PART_A + at : PART_A + stop] = (back * activated).astype(BF16)


def middle(*arrays):
    return run(middle_kernel, [((16, PART_A + PART_B), BF16)], arrays)[0]


def spread_kernel(*refs):
    ins, (out_a, out_b) = refs[:4], refs[4:]
    for j in range(4):
        out_a[pl.ds(16 * j, 16), :] = ins[j][:, :PART_A]
        out_b[pl.ds(16 * j, 16), :] = ins[j][:, PART_A:]


def spread(*arrays):
    return run(spread_kernel, [((64, PART_A), BF16), ((64, PART_B), BF16)], arrays)


def join_kernel(a, came_a, b, came_b, out_a, out_b):
    out_a[:64, :] = a[...]
    out_a[64:, :] = came_a[...]
    out_b[:64, :] = b[...]
    out_b[64:, :] = came_b[...]


def join(*arrays):
    return run(join_kernel, [((128, PART_A), BF16), ((128, PART_B), BF16)], arrays)


def project_kernel(index_a, index_b, a, came_a, b, came_b, gate, up, down, keep, give, sum_a, sum_b):
    left = jnp.concatenate([a[...], came_a[...]], axis=0)
    right = jnp.concatenate([b[...], came_b[...]], axis=0)
    sum_a[:, :512] = nn(left[:, WIDE:], down[:SPLIT, :])
    sum_b[:, :512] = nn(right[:, WIDE:], down[SPLIT:, :])
    sum_a[:, 512:] = nn(left[:, :WIDE], gate[...])
    sum_b[:, 512:] = nn(right[:, :WIDE], up[...])
    for k in range(16):
        out = keep if k < 8 else give
        from_a = pl.multiple_of(index_a[k] * 16, 16)
        from_b = pl.multiple_of(index_b[k] * 16, 16)
        out[pl.ds((k % 8) * 16, 16), :] = (
            sum_a[pl.ds(from_a, 16), :] + sum_b[pl.ds(from_b, 16), :]
        )


def project(*arrays):
    return run(
        project_kernel,
        [((128, 1024), F32)] * 2,
        arrays,
        smem=2,
        scratch=[pltpu.VMEM((256, 1024), F32)] * 2,
        flops=3 * 2 * 256 * 512 * WIDE,
    )


def chunk_kernel(keep_0, came_0, keep_1, came_1, own, *outs):
    for k in range(8):
        rows = pl.ds(16 * k, 16)
        out, at = (outs[k // 2], 32 * (k % 2)) if k < 6 else (outs[3] if k == 6 else own, 0)
        out[pl.ds(at, 16), :] = (keep_0[rows, :] + came_0[rows, :]).astype(out.dtype)
        out[pl.ds(at + 16, 16), :] = (keep_1[rows, :] + came_1[rows, :]).astype(out.dtype)


def chunk(*arrays):
    outs = [((32, 1024), F32)] + [((64, 1024), BF16)] * 3 + [((32, 1024), BF16)]
    return run(chunk_kernel, outs, arrays)


def gather_kernel(own, came_1, came_2, came_3, came_4, mine, other):
    total = [ref[...].astype(F32) for ref in (came_1, came_2, came_3)]
    total = total[0] + total[1] + total[2]
    mine[...] = own[...] + came_4[...].astype(F32) + total[:32]
    other[...] = total[32:]


def gather(*arrays):
    return run(gather_kernel, [((32, 1024), F32)] * 2, arrays)


def finish_kernel(mine, came, output, input_grad):
    output[...] = (mine[:, :512] + came[:, :512]).astype(BF16)
    input_grad[...] = (mine[:, 512:] + came[:, 512:]).astype(BF16)


def finish(*arrays):
    return run(finish_kernel, [((32, 512), BF16)] * 2, arrays)


def weight_grads_kernel(tokens_a, tokens_b, grads_a, grads_b, *refs):
    parts_a, parts_b, (gate, up, down) = refs[:4], refs[4:8], refs[8:11]
    held_a, held_b, wide, tall, came, gone = refs[11:]
    loads = []
    for parts, held in ((parts_a, held_a), (parts_b, held_b)):
        for k in range(4):
            load = pltpu.make_async_copy(
                parts[k], held.at[pl.ds(128 * k, 128), :], came.at[len(loads)]
            )
            load.start()
            loads.append(load)
    stores = []

    def store(source, target):
        copy = pltpu.make_async_copy(source, target, gone.at[len(stores)])
        copy.start()
        stores.append(copy)

    for which, (tokens, grads, held, out, first, last) in enumerate(
        (
            (tokens_a, grads_a, held_a, gate, 0, SPLIT),
            (tokens_b, grads_b, held_b, up, SPLIT, WIDE),
        )
    ):
        turned = jnp.transpose(tokens[...])
        for load in loads[4 * which : 4 * which + 4]:
            load.wait()
        for at, stop in ((0, 512), (512, 1024), (1024, WIDE)):
            columns = pl.ds(at, stop - at)
            wide[which, :, columns] = nn(turned, held[:, columns]).astype(BF16)
            store(wide.at[which, :, columns], out.at[:, columns])
        rows = pl.ds(first, last - first)
        tall[rows, :] = tn(held[:, WIDE:], grads[...]).astype(BF16)
        store(tall.at[rows, :], down.at[rows, :])
    for copy in stores:
        copy.wait()


def weight_grads(*arrays):
    return run(
        weight_grads_kernel,
        [((512, WIDE), BF16), ((512, WIDE), BF16), ((WIDE, 512), BF16)],
        arrays,
        far=range(4, 15),
        scratch=[
            pltpu.VMEM((512, PART_A), BF16),
            pltpu.VMEM((512, PART_B), BF16),
            pltpu.VMEM((2, 512, WIDE), BF16),
            pltpu.VMEM((WIDE, 512), BF16),
            pltpu.SemaphoreType.DMA((8,)),
            pltpu.SemaphoreType.DMA((8,)),
        ],
        flops=3 * 2 * 512 * 512 * WIDE,
    )


def local(tokens, gate_quant, gate_scale, up_quant, up_scale, down_quant, down_scale, out_grad):
    both = stack(tokens, out_grad)
    pair = pair_up(both, lax.ppermute(both, "col", CORES))
    near = [lax.ppermute(pair, "col", fan_by(k)) for k in (3, 2, 1)][::-1]
    four = lax.ppermute(both, "col", turn_by(4))
    pair, row, col, up_quant, gate_quant, down_quant, down_scale = lax.optimization_barrier(
        (pair, lax.axis_index("row"), lax.axis_index("col"))
        + (up_quant, gate_quant, down_quant, down_scale)
    )
    core = lax.rem(col, 2)
    depth = lax.div(col, 2)
    table = jnp.array(
        [[code_of(r // 4, r % 4, c) for c in range(2)] for r in range(16)], jnp.int32
    )
    code = table[row, core]
    blocks = jnp.arange(16, dtype=jnp.int32)

    def swapped(j):
        return (j & 3) | (((j >> 2) & 1) << 3) | (((j >> 3) & 1) << 2)

    def place(group):
        away = (group >> 1) - depth
        slot = jnp.where(core == 0, -away, away) & 7
        return 2 * slot + ((group & 1) ^ core)

    index_a = place(blocks ^ code)
    index_b = place(swapped(blocks) ^ code)
    shift = jnp.array([1, 1, 2, 2, 3, 3, 4, 0] * 2, jnp.int32)
    flip = jnp.array([0, 1, 0, 1, 0, 1, 0, 0] * 2, jnp.int32)
    owner = core ^ (blocks >> 3)
    target = (depth + jnp.where(owner == 0, shift, -shift)) & 7
    home_a = (2 * target + (owner ^ flip)) ^ code
    home_b = swapped(home_a)

    w_up, w_up_turned = scaled(up_scale, up_quant)
    w_gate, w_gate_turned = scaled(gate_scale, gate_quant)
    w_down, w_down_turned = scaled(down_scale, down_quant)
    four, index_a, index_b, home_a, home_b, w_up, w_gate, w_down_turned = lax.optimization_barrier(
        (four, index_a, index_b, home_a, home_b, w_up, w_gate, w_down_turned)
    )
    post = lax.ppermute(stack(*near, four), "col", CORES)
    tokens_a, tokens_b, grads_a, grads_b = arrange(index_a, index_b, pair, *near, four, post)
    parts = first(tokens_a, tokens_b, grads_a, grads_b, w_gate, w_up, w_down_turned)
    state = []
    for part in range(2):
        keep_a, give_a, keep_b, give_b = *parts[2 * part : 2 * part + 2], *parts[4 + 2 * part : 6 + 2 * part]
        state.append((keep_a, send(give_a, 8), keep_b, send(give_b, 4)))
    for part in range(2):
        keep_a, give_a, keep_b, give_b = second(*state[part])
        state[part] = (keep_a, send(give_a, 4), keep_b, send(give_b, 8))
    for part in range(2):
        held, *give = third(*state[part])
        state[part] = (held, *(send(give[j - 1], j) for j in (1, 2, 3)))
    for part in range(2):
        own = middle(*state[part])
        state[part] = (own, *(send(own, j) for j in (1, 2, 3)))
    for part in range(2):
        a, b = spread(*state[part])
        state[part] = (a, send(a, 4), b, send(b, 8))
    for part in range(2):
        a, b = join(*state[part])
        state[part] = (a, send(a, 8), b, send(b, 4))
    ends = []
    for part in range(2):
        keep, give = project(home_a, home_b, *state[part], w_gate_turned, w_up_turned, w_down)
        ends += [keep, lax.ppermute(give, "col", CORES)]
    own, *sent = chunk(*ends)
    own, tokens_a, tokens_b, grads_a, grads_b = lax.optimization_barrier(
        (own, tokens_a, tokens_b, grads_a, grads_b)
    )
    last = [lax.ppermute(sent[k - 1], "col", fan_by(k)) for k in (3, 2, 1)][::-1]
    last.append(lax.ppermute(sent[3], "col", turn_by(4)))
    all_a = [*state[0][:2], *state[1][:2]]
    all_b = [*state[0][2:], *state[1][2:]]
    gate_grad, up_grad, down_grad = weight_grads(
        tokens_a, tokens_b, grads_a, grads_b, *all_a, *all_b
    )
    own, gate_grad, up_grad, down_grad = lax.optimization_barrier(
        (own, gate_grad, up_grad, down_grad)
    )
    mine, other = gather(own, *last)
    output, input_grad = finish(mine, lax.ppermute(other, "col", CORES))
    return (output, input_grad, gate_grad, up_grad, down_grad)


def solution(mesh):
    placed = (
        P("col", "row"),
        P("row", "col"),
        P("row", "col"),
        P("row", "col"),
        P("row", "col"),
        P("col", "row"),
        P("col", "row"),
        P("col", "row"),
    )
    return jax.shard_map(
        local,
        mesh=mesh,
        in_specs=placed,
        out_specs=(
            P("col", "row"),
            P("col", "row"),
            P("row", "col"),
            P("row", "col"),
            P("col", "row"),
        ),
        check_vma=False,
    )
```

```python
import math

import jax
import jax.numpy as jnp
from jax import lax
from jax.experimental import pallas as pl
from jax.experimental.pallas import tpu as pltpu
from jax.sharding import PartitionSpec as P

F32 = jnp.float32
BF16 = jnp.bfloat16
BOTH = ("row", "col")


GRAY_A = (0, 1, 1, 0)
GRAY_B = (0, 0, 1, 1)
WIDE = 1664
SPLIT = 896
PART_A = WIDE + SPLIT
PART_B = WIDE + WIDE - SPLIT
ROOM = 6 * 1024 * 1024
FAR, NEAR = 0, 1


def code_of(y, x, core):
    along_x = 2 * GRAY_A[x] + GRAY_B[x]
    along_y = 2 * GRAY_A[y] + GRAY_B[y]
    return 4 * along_x + along_y if core == 0 else 4 * along_y + along_x


PLACE = {
    (code_of(y, x, core), core): y * 4 + x
    for y in range(4)
    for x in range(4)
    for core in range(2)
}


def flips(mask):
    pairs = []
    for row in range(16):
        for col in range(16):
            code = code_of(row // 4, row % 4, col % 2)
            pairs.append((row * 16 + col, PLACE[(code ^ mask, col % 2)] * 16 + col))
    return pairs


FLIPS = {mask: flips(mask) for mask in (1, 2, 3, 4, 8)}
CORES = [(i, i ^ 1) for i in range(16)]


def turn_by(shift):
    return [(i, (i + 2 * shift) % 16) for i in range(16)]


def fan_by(shift):
    return [(i, (i + (2 - 4 * (i % 2)) * shift) % 16) for i in range(16)]


def send(x, mask):
    return lax.ppermute(x, BOTH, FLIPS[mask])


def tiles(start, stop):
    return [(at, min(at + 256, stop)) for at in range(start, stop, 256)]


def nn(left, right):
    return lax.dot_general(left, right, (((1,), (0,)), ((), ())), preferred_element_type=F32)


def tn(left, right):
    return lax.dot_general(left, right, (((0,), (0,)), ((), ())), preferred_element_type=F32)


def run(kernel, outs, arrays, smem=0, far=(), scratch=(), flops=0):
    shapes = [jax.ShapeDtypeStruct(shape, kind) for shape, kind in outs]
    moved = sum(math.prod(a.shape) * a.dtype.itemsize for a in (*arrays, *shapes))
    held = moved + sum(
        math.prod(s.shape) * jnp.dtype(s.dtype).itemsize for s in scratch if len(s.shape) > 1
    )
    places = [pltpu.SMEM if k < smem else pltpu.VMEM for k in range(len(arrays) + len(outs))]
    for k in far:
        places[k] = pl.ANY
    specs = [pl.BlockSpec(memory_space=place) for place in places]
    return pl.pallas_call(
        kernel,
        out_shape=shapes,
        in_specs=specs[: len(arrays)],
        out_specs=specs[len(arrays) :],
        scratch_shapes=list(scratch),
        compiler_params=pltpu.CompilerParams(vmem_limit_bytes=held + ROOM),
        cost_estimate=pl.CostEstimate(flops=flops, bytes_accessed=moved, transcendentals=0),
    )(*arrays)


def pair_kernel(tokens, grads, other_tokens, other_grads, pair, both, came):
    loads = []
    for which, own in enumerate((tokens, grads)):
        load = pltpu.make_async_copy(own, both.at[pl.ds(32 * which, 32), :], came.at[which])
        load.start()
        loads.append(load)
    for which, other in enumerate((other_tokens, other_grads)):
        pair[pl.ds(64 * which + 32, 32), :] = other[...]
    for which, load in enumerate(loads):
        load.wait()
        pair[pl.ds(64 * which, 32), :] = both[pl.ds(32 * which, 32), :]


def pair_up(*arrays):
    return run(
        pair_kernel,
        [((128, 512), BF16), ((64, 512), BF16)],
        arrays,
        far=range(2),
        scratch=[pltpu.SemaphoreType.DMA((2,))],
    )


def post_kernel(part, *refs):
    ins, post = refs[:-1], refs[-1]
    if part == NEAR:
        near_1, near_2 = ins
        post[pl.ds(0, 128), :] = near_1[...]
        post[pl.ds(128, 32), :] = near_2[pl.ds(32, 32), :]
        post[pl.ds(160, 32), :] = near_2[pl.ds(96, 32), :]
    else:
        near_2, near_3, four = ins
        post[pl.ds(0, 128), :] = near_3[...]
        post[pl.ds(128, 32), :] = near_2[pl.ds(0, 32), :]
        post[pl.ds(160, 32), :] = near_2[pl.ds(64, 32), :]
        post[pl.ds(192, 64), :] = four[...]


def post_up(part, *arrays):
    height = 192 if part == NEAR else 256
    return run(lambda *refs: post_kernel(part, *refs), [((height, 512), BF16)], arrays)[0]


def arrange_kernel(part, index_a, index_b, *refs):
    ins, outs, panel = refs[:-5], refs[-5:-1], refs[-1]
    for which in range(2):
        at, one = 64 * which, 32 * which
        if part == NEAR:
            pair, near_1, near_2, post = ins
            groups = (
                (pair, at),
                (post, at + 32),
                (post, at),
                (post, 128 + one),
                (pair, at + 32),
                (near_1, at + 32),
                (near_1, at),
                (near_2, at + 32),
            )
        else:
            near_2, near_3, four, post = ins
            groups = (
                (post, 128 + one),
                (post, at + 32),
                (post, at),
                (four, one),
                (near_2, at),
                (near_3, at + 32),
                (near_3, at),
                (post, 192 + one),
            )
        for e, (ref, start) in enumerate(groups):
            panel[pl.ds(32 * e, 32), :] = ref[pl.ds(start, 32), :]
        for index, out in zip((index_a, index_b), outs[2 * which : 2 * which + 2]):
            for j in range(16):
                start = pl.multiple_of(index[j] * 16, 16)
                out[pl.ds(16 * j, 16), :] = panel[pl.ds(start, 16), :]


def arrange(part, *arrays):
    return run(
        lambda *refs: arrange_kernel(part, *refs),
        [((256, 512), BF16)] * 4,
        arrays,
        smem=2,
        scratch=[pltpu.VMEM((256, 512), BF16)],
    )


def scale_kernel(scale, quant, weight, turned):
    block_rows, block_columns = scale.shape
    for r in range(block_rows):
        for c in range(block_columns):
            rows, columns = pl.ds(r * 128, 128), pl.ds(c * 128, 128)
            block = (quant[rows, columns].astype(F32) * scale[r, c]).astype(BF16)
            weight[rows, columns] = block
            turned[columns, rows] = jnp.transpose(block)


def scaled(scale, quant):
    outs = [(quant.shape, BF16), (quant.shape[::-1], BF16)]
    return run(scale_kernel, outs, [scale, quant], smem=1)


def first_kernel(tokens_a, tokens_b, grads_a, grads_b, gate, up, down, *outs):
    a, b = outs[:2], outs[2:]
    for panel, weight, first, last, shift, (keep, give) in (
        (tokens_a, gate, 0, WIDE, 0, a),
        (tokens_b, up, 0, WIDE, 0, b),
        (grads_a, down, 0, SPLIT, WIDE, a),
        (grads_b, down, SPLIT, WIDE, WIDE - SPLIT, b),
    ):
        for at, stop in tiles(first, last):
            product = nn(panel[...], weight[:, at:stop])
            columns = pl.ds(at + shift, stop - at)
            keep[:, columns] = product[:128]
            give[:, columns] = product[128:].astype(BF16)


def first(*arrays):
    outs = [((128, width), kind) for width in (PART_A, PART_B) for kind in (F32, BF16)]
    return run(first_kernel, outs, arrays, flops=3 * 2 * 256 * 512 * WIDE)


def second_kernel(held_a, came_a, held_b, came_b, keep_a, give_a, keep_b, give_b):
    for held, came, keep, give in (
        (held_a, came_a, keep_a, give_a),
        (held_b, came_b, keep_b, give_b),
    ):
        keep[...] = held[:64] + came[:64].astype(F32)
        give[...] = (held[64:] + came[64:].astype(F32)).astype(give.dtype)


def second(*arrays):
    outs = [((64, width), kind) for width in (PART_A, PART_B) for kind in (F32, BF16)]
    return run(second_kernel, outs, arrays)


def third_kernel(held_a, came_a, held_b, came_b, *outs):
    for j in range(4):
        rows = pl.ds(16 * j, 16)
        outs[j][:, :PART_A] = held_a[rows, :] + came_a[rows, :].astype(F32)
        outs[j][:, PART_A:] = held_b[rows, :] + came_b[rows, :].astype(F32)


def third(*arrays):
    return run(third_kernel, [((16, PART_A + PART_B), F32)] * 4, arrays)


def middle_kernel(held, came_1, came_2, came_3, out):
    def total(at, stop):
        return (held[:, at:stop] + came_1[:, at:stop]) + (came_2[:, at:stop] + came_3[:, at:stop])

    for at, stop in [(0, SPLIT), (SPLIT, WIDE)]:
        gate = total(at, stop)
        up = total(PART_A + at, PART_A + stop)
        offset = WIDE if at == 0 else PART_A + WIDE - SPLIT
        back = total(offset + at, offset + stop)
        sigmoid = 1.0 / (1.0 + jnp.exp(-gate))
        activated = gate * sigmoid
        out[:, offset + at : offset + stop] = (activated * up).astype(BF16)
        slope = sigmoid * (1.0 + gate * (1.0 - sigmoid))
        out[:, at:stop] = (back * up * slope).astype(BF16)
        out[:, PART_A + at : PART_A + stop] = (back * activated).astype(BF16)


def middle(*arrays):
    return run(middle_kernel, [((16, PART_A + PART_B), BF16)], arrays)[0]


def spread_kernel(*refs):
    ins, (out_a, out_b) = refs[:4], refs[4:]
    for j in range(4):
        out_a[pl.ds(16 * j, 16), :] = ins[j][:, :PART_A]
        out_b[pl.ds(16 * j, 16), :] = ins[j][:, PART_A:]


def spread(*arrays):
    return run(spread_kernel, [((64, PART_A), BF16), ((64, PART_B), BF16)], arrays)


def join_kernel(a, came_a, b, came_b, out_a, out_b):
    out_a[:64, :] = a[...]
    out_a[64:, :] = came_a[...]
    out_b[:64, :] = b[...]
    out_b[64:, :] = came_b[...]


def join(*arrays):
    return run(join_kernel, [((128, PART_A), BF16), ((128, PART_B), BF16)], arrays)


def project_kernel(index_a, index_b, a, came_a, b, came_b, gate, up, down, keep, give, sum_a, sum_b):
    left = jnp.concatenate([a[...], came_a[...]], axis=0)
    right = jnp.concatenate([b[...], came_b[...]], axis=0)
    sum_a[:, :512] = nn(left[:, WIDE:], down[:SPLIT, :])
    sum_b[:, :512] = nn(right[:, WIDE:], down[SPLIT:, :])
    sum_a[:, 512:] = nn(left[:, :WIDE], gate[...])
    sum_b[:, 512:] = nn(right[:, :WIDE], up[...])
    for k in range(16):
        out = keep if k < 8 else give
        from_a = pl.multiple_of(index_a[k] * 16, 16)
        from_b = pl.multiple_of(index_b[k] * 16, 16)
        out[pl.ds((k % 8) * 16, 16), :] = (
            sum_a[pl.ds(from_a, 16), :] + sum_b[pl.ds(from_b, 16), :]
        )


def project(*arrays):
    return run(
        project_kernel,
        [((128, 1024), F32)] * 2,
        arrays,
        smem=2,
        scratch=[pltpu.VMEM((256, 1024), F32)] * 2,
        flops=3 * 2 * 256 * 512 * WIDE,
    )


def chunk_kernel(keep, came, *outs):
    at = 0
    for out in outs:
        rows = pl.ds(at, out.shape[0])
        out[...] = (keep[rows, :] + came[rows, :]).astype(out.dtype)
        at += out.shape[0]


def chunk(part, *arrays):
    heights = ((32, BF16), (64, BF16), (32, BF16))
    if part == NEAR:
        heights = ((32, F32), (64, BF16), (32, BF16))
    return run(chunk_kernel, [((rows, 1024), kind) for rows, kind in heights], arrays)


def gather_kernel(own, came_1, came_2, far_2, far_3, far_4, mine, other):
    two = (came_1[...].astype(F32), far_3[...].astype(F32))
    total = own[...] + far_4[...].astype(F32) + came_2[...].astype(F32)
    mine[...] = total + (two[0][:32] + two[1][:32])
    other[...] = far_2[...].astype(F32) + (two[0][32:] + two[1][32:])


def gather(*arrays):
    return run(gather_kernel, [((32, 1024), F32)] * 2, arrays)


def finish_kernel(mine, came, output, input_grad):
    output[...] = (mine[:, :512] + came[:, :512]).astype(BF16)
    input_grad[...] = (mine[:, 512:] + came[:, 512:]).astype(BF16)


def finish(*arrays):
    return run(finish_kernel, [((32, 512), BF16)] * 2, arrays)


def weight_grads_kernel(*refs):
    panels, parts_a, parts_b, (gate, up, down) = refs[:8], refs[8:12], refs[12:16], refs[16:19]
    held_a, held_b, wide, tall, came, gone = refs[19:]

    def whole(k):
        return jnp.concatenate([panels[k][...], panels[k + 4][...]], axis=0)

    loads = []
    for parts, held in ((parts_a, held_a), (parts_b, held_b)):
        for k in range(4):
            load = pltpu.make_async_copy(
                parts[k], held.at[pl.ds(128 * k, 128), :], came.at[len(loads)]
            )
            load.start()
            loads.append(load)
    stores = []

    def store(source, target):
        copy = pltpu.make_async_copy(source, target, gone.at[len(stores)])
        copy.start()
        stores.append(copy)

    for which, (tokens, grads, held, out, first, last) in enumerate(
        (
            (whole(0), whole(2), held_a, gate, 0, SPLIT),
            (whole(1), whole(3), held_b, up, SPLIT, WIDE),
        )
    ):
        turned = jnp.transpose(tokens)
        for load in loads[4 * which : 4 * which + 4]:
            load.wait()
        for at, stop in ((0, 512), (512, 1024), (1024, WIDE)):
            columns = pl.ds(at, stop - at)
            wide[which, :, columns] = nn(turned, held[:, columns]).astype(BF16)
            store(wide.at[which, :, columns], out.at[:, columns])
        rows = pl.ds(first, last - first)
        tall[rows, :] = tn(held[:, WIDE:], grads).astype(BF16)
        store(tall.at[rows, :], down.at[rows, :])
    for copy in stores:
        copy.wait()


def weight_grads(*arrays):
    return run(
        weight_grads_kernel,
        [((512, WIDE), BF16), ((512, WIDE), BF16), ((WIDE, 512), BF16)],
        arrays,
        far=range(8, 19),
        scratch=[
            pltpu.VMEM((512, PART_A), BF16),
            pltpu.VMEM((512, PART_B), BF16),
            pltpu.VMEM((2, 512, WIDE), BF16),
            pltpu.VMEM((WIDE, 512), BF16),
            pltpu.SemaphoreType.DMA((8,)),
            pltpu.SemaphoreType.DMA((8,)),
        ],
        flops=3 * 2 * 512 * 512 * WIDE,
    )


def local(tokens, gate_quant, gate_scale, up_quant, up_scale, down_quant, down_scale, out_grad):
    pair, both = pair_up(
        tokens, out_grad, *(lax.ppermute(x, "col", CORES) for x in (tokens, out_grad))
    )
    near_1, near_2, near_3 = (lax.ppermute(pair, "col", fan_by(k)) for k in (1, 2, 3))
    four = lax.ppermute(both, "col", turn_by(4))
    pair, row, col, up_quant, gate_quant, down_quant, down_scale = lax.optimization_barrier(
        (pair, lax.axis_index("row"), lax.axis_index("col"))
        + (up_quant, gate_quant, down_quant, down_scale)
    )
    table = jnp.array(
        [[code_of(r // 4, r % 4, c) for c in range(2)] for r in range(16)], jnp.int32
    )
    code = table[row, lax.rem(col, 2)]
    blocks = jnp.arange(16, dtype=jnp.int32)

    def swapped(j):
        return (j & 3) | (((j >> 2) & 1) << 3) | (((j >> 3) & 1) << 2)

    index_a = blocks ^ code
    index_b = swapped(blocks) ^ code
    home_b = swapped(index_a)
    w_up, w_up_turned = scaled(up_scale, up_quant)
    w_gate, w_gate_turned = scaled(gate_scale, gate_quant)
    w_down, w_down_turned = scaled(down_scale, down_quant)
    near_1, near_2, near_3, four, index_a, index_b, home_b, w_up, w_gate, w_down_turned = (
        lax.optimization_barrier(
            (near_1, near_2, near_3, four, index_a, index_b, home_b, w_up, w_gate, w_down_turned)
        )
    )
    panels, state = [], []
    for part, pieces in enumerate(((near_2, near_3, four), (near_1, near_2))):
        post = lax.ppermute(post_up(part, *pieces), "col", CORES)
        lead = (pair,) if part == NEAR else ()
        panel = arrange(part, index_a, index_b, *lead, *pieces, post)
        keep_a, give_a, keep_b, give_b = first(*panel, w_gate, w_up, w_down_turned)
        panels += panel
        state.append((keep_a, send(give_a, 8), keep_b, send(give_b, 4)))
    for part in range(2):
        keep_a, give_a, keep_b, give_b = second(*state[part])
        state[part] = (keep_a, send(give_a, 4), keep_b, send(give_b, 8))
    for part in range(2):
        held, *give = third(*state[part])
        state[part] = (held, *(send(give[j - 1], j) for j in (1, 2, 3)))
    for part in range(2):
        own = middle(*state[part])
        state[part] = (own, *(send(own, j) for j in (1, 2, 3)))
    for part in range(2):
        a, b = spread(*state[part])
        state[part] = (a, send(a, 4), b, send(b, 8))
    for part in range(2):
        a, b = join(*state[part])
        state[part] = (a, send(a, 8), b, send(b, 4))
    weights = (w_gate_turned, w_up_turned, w_down)
    keep, give = project(index_a, home_b, *state[FAR], *weights)
    far = chunk(FAR, keep, lax.ppermute(give, "col", CORES))
    far_2, far_3 = (lax.ppermute(far[k - 2], "col", fan_by(k)) for k in (2, 3))
    far_4 = lax.ppermute(far[2], "col", turn_by(4))
    keep, give = project(index_a, home_b, *state[NEAR], *weights)
    own, *near = chunk(NEAR, keep, lax.ppermute(give, "col", CORES))
    own, *panels = lax.optimization_barrier((own, *panels))
    last = [lax.ppermute(near[k - 1], "col", fan_by(k)) for k in (1, 2)] + [far_2, far_3, far_4]
    all_a = [*state[0][:2], *state[1][:2]]
    all_b = [*state[0][2:], *state[1][2:]]
    gate_grad, up_grad, down_grad = weight_grads(*panels, *all_a, *all_b)
    own, gate_grad, up_grad, down_grad = lax.optimization_barrier(
        (own, gate_grad, up_grad, down_grad)
    )
    mine, other = gather(own, *last)
    output, input_grad = finish(mine, lax.ppermute(other, "col", CORES))
    return (output, input_grad, gate_grad, up_grad, down_grad)


def solution(mesh):
    placed = (
        P("col", "row"),
        P("row", "col"),
        P("row", "col"),
        P("row", "col"),
        P("row", "col"),
        P("col", "row"),
        P("col", "row"),
        P("col", "row"),
    )
    return jax.shard_map(
        local,
        mesh=mesh,
        in_specs=placed,
        out_specs=(
            P("col", "row"),
            P("col", "row"),
            P("row", "col"),
            P("row", "col"),
            P("col", "row"),
        ),
        check_vma=False,
    )
```

```python
import math

import jax
import jax.numpy as jnp
from jax import lax
from jax.experimental import pallas as pl
from jax.experimental.pallas import tpu as pltpu
from jax.sharding import PartitionSpec as P

F32 = jnp.float32
BF16 = jnp.bfloat16
BOTH = ("row", "col")


GRAY_A = (0, 1, 1, 0)
GRAY_B = (0, 0, 1, 1)
WIDE = 1664
SPLIT = 896
PART_A = WIDE + SPLIT
PART_B = WIDE + WIDE - SPLIT
ROOM = 6 * 1024 * 1024


def code_of(y, x, core):
    along_x = 2 * GRAY_A[x] + GRAY_B[x]
    along_y = 2 * GRAY_A[y] + GRAY_B[y]
    return 4 * along_x + along_y if core == 0 else 4 * along_y + along_x


PLACE = {
    (code_of(y, x, core), core): y * 4 + x
    for y in range(4)
    for x in range(4)
    for core in range(2)
}


def flips(mask):
    pairs = []
    for row in range(16):
        for col in range(16):
            code = code_of(row // 4, row % 4, col % 2)
            pairs.append((row * 16 + col, PLACE[(code ^ mask, col % 2)] * 16 + col))
    return pairs


FLIPS = {mask: flips(mask) for mask in (1, 2, 3, 4, 8)}
CORES = [(i, i ^ 1) for i in range(16)]


def turn_by(shift):
    return [(i, (i + 2 * shift) % 16) for i in range(16)]


def fan_by(shift):
    return [(i, (i + (2 - 4 * (i % 2)) * shift) % 16) for i in range(16)]


def send(x, mask):
    return lax.ppermute(x, BOTH, FLIPS[mask])


def tiles(start, stop):
    return [(at, min(at + 256, stop)) for at in range(start, stop, 256)]


def nn(left, right):
    return lax.dot_general(left, right, (((1,), (0,)), ((), ())), preferred_element_type=F32)


def tn(left, right):
    return lax.dot_general(left, right, (((0,), (0,)), ((), ())), preferred_element_type=F32)


def run(kernel, outs, arrays, smem=0, far=(), scratch=(), flops=0):
    shapes = [jax.ShapeDtypeStruct(shape, kind) for shape, kind in outs]
    moved = sum(math.prod(a.shape) * a.dtype.itemsize for a in (*arrays, *shapes))
    held = moved + sum(
        math.prod(s.shape) * jnp.dtype(s.dtype).itemsize for s in scratch if len(s.shape) > 1
    )
    places = [pltpu.SMEM if k < smem else pltpu.VMEM for k in range(len(arrays) + len(outs))]
    for k in far:
        places[k] = pl.ANY
    specs = [pl.BlockSpec(memory_space=place) for place in places]
    return pl.pallas_call(
        kernel,
        out_shape=shapes,
        in_specs=specs[: len(arrays)],
        out_specs=specs[len(arrays) :],
        scratch_shapes=list(scratch),
        compiler_params=pltpu.CompilerParams(vmem_limit_bytes=held + ROOM),
        cost_estimate=pl.CostEstimate(flops=flops, bytes_accessed=moved, transcendentals=0),
    )(*arrays)


def stack_kernel(*refs):
    at = 0
    for ref in refs[:-1]:
        refs[-1][pl.ds(at, ref.shape[0]), :] = ref[...]
        at += ref.shape[0]


def stack(*arrays):
    height = sum(a.shape[0] for a in arrays)
    return run(stack_kernel, [((height, arrays[0].shape[1]), arrays[0].dtype)], arrays)[0]


def pair_kernel(both, other, out):
    for which in range(2):
        rows = pl.ds(32 * which, 32)
        out[pl.ds(64 * which, 32), :] = both[rows, :]
        out[pl.ds(64 * which + 32, 32), :] = other[rows, :]


def pair_up(*arrays):
    return run(pair_kernel, [((128, 512), BF16)], arrays)[0]


def arrange_kernel(part, index_a, index_b, *refs):
    ins, outs, panel = refs[:-5], refs[-5:-1], refs[-1]
    for which in range(2):
        at, one = 64 * which, 32 * which
        if part == 0:
            pair, near_1, near_2, post = ins
            groups = (
                (pair, at),
                (post, at + 32),
                (post, at),
                (post, 128 + at + 32),
                (pair, at + 32),
                (near_1, at + 32),
                (near_1, at),
                (near_2, at + 32),
            )
        else:
            near_2, near_3, four, post = ins
            groups = (
                (post, 128 + at),
                (post, 256 + at + 32),
                (post, 256 + at),
                (four, one),
                (near_2, at),
                (near_3, at + 32),
                (near_3, at),
                (post, 384 + one),
            )
        for e, (ref, start) in enumerate(groups):
            panel[pl.ds(32 * e, 32), :] = ref[pl.ds(start, 32), :]
        for index, out in zip((index_a, index_b), outs[2 * which : 2 * which + 2]):
            for j in range(16):
                start = pl.multiple_of(index[j] * 16, 16)
                out[pl.ds(16 * j, 16), :] = panel[pl.ds(start, 16), :]


def arrange(part, *arrays):
    return run(
        lambda *refs: arrange_kernel(part, *refs),
        [((256, 512), BF16)] * 4,
        arrays,
        smem=2,
        scratch=[pltpu.VMEM((256, 512), BF16)],
    )


def scale_kernel(scale, quant, weight, turned):
    block_rows, block_columns = scale.shape
    for r in range(block_rows):
        for c in range(block_columns):
            rows, columns = pl.ds(r * 128, 128), pl.ds(c * 128, 128)
            block = (quant[rows, columns].astype(F32) * scale[r, c]).astype(BF16)
            weight[rows, columns] = block
            turned[columns, rows] = jnp.transpose(block)


def scaled(scale, quant):
    outs = [(quant.shape, BF16), (quant.shape[::-1], BF16)]
    return run(scale_kernel, outs, [scale, quant], smem=1)


def first_kernel(tokens_a, tokens_b, grads_a, grads_b, gate, up, down, *outs):
    a, b = outs[:2], outs[2:]
    for panel, weight, first, last, shift, (keep, give) in (
        (tokens_a, gate, 0, WIDE, 0, a),
        (tokens_b, up, 0, WIDE, 0, b),
        (grads_a, down, 0, SPLIT, WIDE, a),
        (grads_b, down, SPLIT, WIDE, WIDE - SPLIT, b),
    ):
        for at, stop in tiles(first, last):
            product = nn(panel[...], weight[:, at:stop])
            columns = pl.ds(at + shift, stop - at)
            keep[:, columns] = product[:128]
            give[:, columns] = product[128:].astype(BF16)


def first(*arrays):
    outs = [((128, width), kind) for width in (PART_A, PART_B) for kind in (F32, BF16)]
    return run(first_kernel, outs, arrays, flops=3 * 2 * 256 * 512 * WIDE)


def second_kernel(held_a, came_a, held_b, came_b, keep_a, give_a, keep_b, give_b):
    for held, came, keep, give in (
        (held_a, came_a, keep_a, give_a),
        (held_b, came_b, keep_b, give_b),
    ):
        keep[...] = held[:64] + came[:64].astype(F32)
        give[...] = (held[64:] + came[64:].astype(F32)).astype(give.dtype)


def second(*arrays):
    outs = [((64, width), kind) for width in (PART_A, PART_B) for kind in (F32, BF16)]
    return run(second_kernel, outs, arrays)


def third_kernel(held_a, came_a, held_b, came_b, *outs):
    for j in range(4):
        rows = pl.ds(16 * j, 16)
        outs[j][:, :PART_A] = held_a[rows, :] + came_a[rows, :].astype(F32)
        outs[j][:, PART_A:] = held_b[rows, :] + came_b[rows, :].astype(F32)


def third(*arrays):
    return run(third_kernel, [((16, PART_A + PART_B), F32)] * 4, arrays)


def middle_kernel(held, came_1, came_2, came_3, out):
    def total(at, stop):
        return (held[:, at:stop] + came_1[:, at:stop]) + (came_2[:, at:stop] + came_3[:, at:stop])

    for at, stop in [(0, SPLIT), (SPLIT, WIDE)]:
        gate = total(at, stop)
        up = total(PART_A + at, PART_A + stop)
        offset = WIDE if at == 0 else PART_A + WIDE - SPLIT
        back = total(offset + at, offset + stop)
        sigmoid = 1.0 / (1.0 + jnp.exp(-gate))
        activated = gate * sigmoid
        out[:, offset + at : offset + stop] = (activated * up).astype(BF16)
        slope = sigmoid * (1.0 + gate * (1.0 - sigmoid))
        out[:, at:stop] = (back * up * slope).astype(BF16)
        out[:, PART_A + at : PART_A + stop] = (back * activated).astype(BF16)


def middle(*arrays):
    return run(middle_kernel, [((16, PART_A + PART_B), BF16)], arrays)[0]


def spread_kernel(*refs):
    ins, (out_a, out_b) = refs[:4], refs[4:]
    for j in range(4):
        out_a[pl.ds(16 * j, 16), :] = ins[j][:, :PART_A]
        out_b[pl.ds(16 * j, 16), :] = ins[j][:, PART_A:]


def spread(*arrays):
    return run(spread_kernel, [((64, PART_A), BF16), ((64, PART_B), BF16)], arrays)


def join_kernel(a, came_a, b, came_b, out_a, out_b):
    out_a[:64, :] = a[...]
    out_a[64:, :] = came_a[...]
    out_b[:64, :] = b[...]
    out_b[64:, :] = came_b[...]


def join(*arrays):
    return run(join_kernel, [((128, PART_A), BF16), ((128, PART_B), BF16)], arrays)


def project_kernel(index_a, index_b, a, came_a, b, came_b, gate, up, down, keep, give, sum_a, sum_b):
    left = jnp.concatenate([a[...], came_a[...]], axis=0)
    right = jnp.concatenate([b[...], came_b[...]], axis=0)
    sum_a[:, :512] = nn(left[:, WIDE:], down[:SPLIT, :])
    sum_b[:, :512] = nn(right[:, WIDE:], down[SPLIT:, :])
    sum_a[:, 512:] = nn(left[:, :WIDE], gate[...])
    sum_b[:, 512:] = nn(right[:, :WIDE], up[...])
    for k in range(16):
        out = keep if k < 8 else give
        from_a = pl.multiple_of(index_a[k] * 16, 16)
        from_b = pl.multiple_of(index_b[k] * 16, 16)
        out[pl.ds((k % 8) * 16, 16), :] = (
            sum_a[pl.ds(from_a, 16), :] + sum_b[pl.ds(from_b, 16), :]
        )


def project(*arrays):
    return run(
        project_kernel,
        [((128, 1024), F32)] * 2,
        arrays,
        smem=2,
        scratch=[pltpu.VMEM((256, 1024), F32)] * 2,
        flops=3 * 2 * 256 * 512 * WIDE,
    )


def chunk_kernel(keep_0, came_0, keep_1, came_1, own, out_1, out_2, out_3, out_4):
    for out, at, keep, came, start in (
        (own, 0, keep_0, came_0, 0),
        (out_1, 0, keep_0, came_0, 32),
        (out_1, 32, keep_0, came_0, 64),
        (out_2, 0, keep_0, came_0, 96),
        (out_2, 32, keep_1, came_1, 0),
        (out_3, 0, keep_1, came_1, 32),
        (out_3, 32, keep_1, came_1, 64),
        (out_4, 0, keep_1, came_1, 96),
    ):
        rows = pl.ds(start, 32)
        out[pl.ds(at, 32), :] = (keep[rows, :] + came[rows, :]).astype(out.dtype)


def chunk(*arrays):
    outs = [((32, 1024), F32)] + [((64, 1024), BF16)] * 3 + [((32, 1024), BF16)]
    return run(chunk_kernel, outs, arrays)


def gather_kernel(own, came_1, came_2, came_3, came_4, mine, other):
    total = [ref[...].astype(F32) for ref in (came_1, came_2, came_3)]
    total = total[0] + total[1] + total[2]
    mine[...] = own[...] + came_4[...].astype(F32) + total[:32]
    other[...] = total[32:]


def gather(*arrays):
    return run(gather_kernel, [((32, 1024), F32)] * 2, arrays)


def finish_kernel(mine, came, output, input_grad):
    output[...] = (mine[:, :512] + came[:, :512]).astype(BF16)
    input_grad[...] = (mine[:, 512:] + came[:, 512:]).astype(BF16)


def finish(*arrays):
    return run(finish_kernel, [((32, 512), BF16)] * 2, arrays)


def weight_grads_kernel(*refs):
    panels, parts_a, parts_b, (gate, up, down) = refs[:8], refs[8:12], refs[12:16], refs[16:19]
    held_a, held_b, wide, tall, came, gone = refs[19:]

    def whole(k):
        return jnp.concatenate([panels[k][...], panels[k + 4][...]], axis=0)

    loads = []
    for parts, held in ((parts_a, held_a), (parts_b, held_b)):
        for k in range(4):
            load = pltpu.make_async_copy(
                parts[k], held.at[pl.ds(128 * k, 128), :], came.at[len(loads)]
            )
            load.start()
            loads.append(load)
    stores = []

    def store(source, target):
        copy = pltpu.make_async_copy(source, target, gone.at[len(stores)])
        copy.start()
        stores.append(copy)

    for which, (tokens, grads, held, out, first, last) in enumerate(
        (
            (whole(0), whole(2), held_a, gate, 0, SPLIT),
            (whole(1), whole(3), held_b, up, SPLIT, WIDE),
        )
    ):
        turned = jnp.transpose(tokens)
        for load in loads[4 * which : 4 * which + 4]:
            load.wait()
        for at, stop in ((0, 512), (512, 1024), (1024, WIDE)):
            columns = pl.ds(at, stop - at)
            wide[which, :, columns] = nn(turned, held[:, columns]).astype(BF16)
            store(wide.at[which, :, columns], out.at[:, columns])
        rows = pl.ds(first, last - first)
        tall[rows, :] = tn(held[:, WIDE:], grads).astype(BF16)
        store(tall.at[rows, :], down.at[rows, :])
    for copy in stores:
        copy.wait()


def weight_grads(*arrays):
    return run(
        weight_grads_kernel,
        [((512, WIDE), BF16), ((512, WIDE), BF16), ((WIDE, 512), BF16)],
        arrays,
        far=range(8, 19),
        scratch=[
            pltpu.VMEM((512, PART_A), BF16),
            pltpu.VMEM((512, PART_B), BF16),
            pltpu.VMEM((2, 512, WIDE), BF16),
            pltpu.VMEM((WIDE, 512), BF16),
            pltpu.SemaphoreType.DMA((8,)),
            pltpu.SemaphoreType.DMA((8,)),
        ],
        flops=3 * 2 * 512 * 512 * WIDE,
    )


def local(tokens, gate_quant, gate_scale, up_quant, up_scale, down_quant, down_scale, out_grad):
    both = stack(tokens, out_grad)
    pair = pair_up(both, lax.ppermute(both, "col", CORES))
    near_1, near_2, near_3 = (lax.ppermute(pair, "col", fan_by(k)) for k in (1, 2, 3))
    four = lax.ppermute(both, "col", turn_by(4))
    pair, row, col, up_quant, gate_quant, down_quant, down_scale = lax.optimization_barrier(
        (pair, lax.axis_index("row"), lax.axis_index("col"))
        + (up_quant, gate_quant, down_quant, down_scale)
    )
    table = jnp.array(
        [[code_of(r // 4, r % 4, c) for c in range(2)] for r in range(16)], jnp.int32
    )
    code = table[row, lax.rem(col, 2)]
    blocks = jnp.arange(16, dtype=jnp.int32)

    def swapped(j):
        return (j & 3) | (((j >> 2) & 1) << 3) | (((j >> 3) & 1) << 2)

    index_a = blocks ^ code
    index_b = swapped(blocks) ^ code
    home_b = swapped(index_a)
    w_up, w_up_turned = scaled(up_scale, up_quant)
    w_gate, w_gate_turned = scaled(gate_scale, gate_quant)
    w_down, w_down_turned = scaled(down_scale, down_quant)
    near_1, near_2, near_3, four, index_a, index_b, home_b, w_up, w_gate, w_down_turned = (
        lax.optimization_barrier(
            (near_1, near_2, near_3, four, index_a, index_b, home_b, w_up, w_gate, w_down_turned)
        )
    )
    post = lax.ppermute(stack(near_1, near_2, near_3, four), "col", CORES)
    panels, state = [], []
    for part, pieces in enumerate(((near_1, near_2), (near_2, near_3, four))):
        lead = (pair,) if part == 0 else ()
        panel = arrange(part, index_a, index_b, *lead, *pieces, post)
        keep_a, give_a, keep_b, give_b = first(*panel, w_gate, w_up, w_down_turned)
        panels += panel
        state.append((keep_a, send(give_a, 8), keep_b, send(give_b, 4)))
    for part in range(2):
        keep_a, give_a, keep_b, give_b = second(*state[part])
        state[part] = (keep_a, send(give_a, 4), keep_b, send(give_b, 8))
    for part in range(2):
        held, *give = third(*state[part])
        state[part] = (held, *(send(give[j - 1], j) for j in (1, 2, 3)))
    for part in range(2):
        own = middle(*state[part])
        state[part] = (own, *(send(own, j) for j in (1, 2, 3)))
    for part in range(2):
        a, b = spread(*state[part])
        state[part] = (a, send(a, 4), b, send(b, 8))
    for part in range(2):
        a, b = join(*state[part])
        state[part] = (a, send(a, 8), b, send(b, 4))
    ends = []
    for part in range(2):
        keep, give = project(index_a, home_b, *state[part], w_gate_turned, w_up_turned, w_down)
        ends += [keep, lax.ppermute(give, "col", CORES)]
    own, *sent = chunk(*ends)
    own, *panels = lax.optimization_barrier((own, *panels))
    last = [lax.ppermute(sent[k - 1], "col", fan_by(k)) for k in (3, 2, 1)][::-1]
    last.append(lax.ppermute(sent[3], "col", turn_by(4)))
    all_a = [*state[0][:2], *state[1][:2]]
    all_b = [*state[0][2:], *state[1][2:]]
    gate_grad, up_grad, down_grad = weight_grads(*panels, *all_a, *all_b)
    own, gate_grad, up_grad, down_grad = lax.optimization_barrier(
        (own, gate_grad, up_grad, down_grad)
    )
    mine, other = gather(own, *last)
    output, input_grad = finish(mine, lax.ppermute(other, "col", CORES))
    return (output, input_grad, gate_grad, up_grad, down_grad)


def solution(mesh):
    placed = (
        P("col", "row"),
        P("row", "col"),
        P("row", "col"),
        P("row", "col"),
        P("row", "col"),
        P("col", "row"),
        P("col", "row"),
        P("col", "row"),
    )
    return jax.shard_map(
        local,
        mesh=mesh,
        in_specs=placed,
        out_specs=(
            P("col", "row"),
            P("col", "row"),
            P("row", "col"),
            P("row", "col"),
            P("col", "row"),
        ),
        check_vma=False,
    )
```
